256 devices in a mesh: srow: 8 (over z_lo, y), scol: 8 (over x, core), hour: 4 (over z_hi).
Axes of the slice: x: 4, y: 4, z: 8 (z_hi: 4, z_lo: 2; z = z_hi * 2 + z_lo), core: 2. Of those that a mesh axis runs over, the one named last changes fastest.
Arguments:
- readings: bfloat16 [32768, 4608], P(('srow', 'scol'), 'hour'), may hold values from -18 to 18
- space_basis: bfloat16 [32768, 32768], P('srow', ('scol', 'hour')), may hold values from -0.0625 to 0.0625
- time_modes: bfloat16 [4608, 512], P('hour'), may hold values from -0.09375 to 0.09375
- space_power: float32 [32768], P(('scol', 'hour')), may hold values from 0.05 to 20
- time_power: float32 [512], replicated, may hold values from 0.05 to 20
Outputs:
- posterior: bfloat16 [32768, 4608], P(('srow', 'scol'), 'hour')
The draws below stay inside these ranges and needn't reach their ends.
All inputs are finite; a program needn't handle non-finite values.
Results may differ from the reference program's by a relative error of at most 0.0065.
Values may be sent and summed in bfloat16 or wider, within the bound.
A program may use at most 64 MiB of HBM per device.

```python
import math
import jax
import jax.numpy as jnp
from jax import lax

S = 32768
H = 4608
MODES = 512


def spiked(array, own_key, source, target, blocks, factor):
    def block_of(axis_at):
        return (jnp.arange(array.shape[axis_at]) // (array.shape[axis_at] // blocks)).reshape((-1,) + (1,) * (array.ndim - 1 - axis_at))

    one_side = jax.random.permutation(own_key, blocks)[block_of(target)]
    second = (block_of(target) + blocks // 2) % blocks
    return jnp.where((block_of(source) == one_side) | (block_of(source) == second), factor * array, array)


def shard_levels(stream_key, extent, split, smallest, largest):
    level, own = 1.0, jax.random.fold_in(stream_key, 6)
    for dim, parts in split:
        draws = jnp.exp(jax.random.uniform(jax.random.fold_in(own, dim), (parts,), jnp.float32, smallest / len(split), largest / len(split)))
        level = level * jnp.repeat(draws, extent[dim] // parts).reshape([-1 if axis == dim else 1 for axis in range(len(extent))])
    return level


def centred(key, dims, scale, limit, cuts=(), dtype=jnp.bfloat16):
    gain = shard_levels(key, dims, cuts, -0.22, 0.18) if cuts else 1.0
    array = jax.random.normal(key, dims, jnp.float32) * scale * gain
    return jnp.minimum(jnp.maximum(array, -limit), limit).astype(dtype)


def noise_with(key, dims, spread, bound, pieces, heavy, dtype=jnp.bfloat16):
    entries = spread * jax.random.normal(key, dims, jnp.float32)
    if pieces:
        entries = entries * shard_levels(key, dims, pieces, -0.22, 0.18)
    return jnp.clip(spiked(entries, jax.random.fold_in(key, 3), *heavy), -bound, bound).astype(dtype)


def setup_inputs(seed: int = 0) -> dict:
    key_list = jax.random.split(jax.random.key(seed), 6)
    readings = centred(key_list[0], (S, H), 3.0, 18.0, ((0, 64), (1, 4)))
    space_basis = noise_with(key_list[1], (S, S), S ** -0.5, 0.0625, ((0, 8), (1, 32)), (1, 0, 32, 2.75))
    time_modes = centred(key_list[2], (H, MODES), H ** -0.5, 0.09375, ((0, 4),))
    space_power = jnp.clip(jnp.exp(math.log(20.0) - 5.9914645 * jax.random.uniform(key_list[3], (S,), jnp.float32) ** shard_levels(key_list[3], (S,), ((0, 32),), -0.2, 0.2)), 0.05, 20.0)
    time_power = jnp.clip(jnp.exp(jax.random.uniform(key_list[4], (MODES,), jnp.float32, math.log(0.05), math.log(20.0))), 0.05, 20.0)
    return dict(readings=readings, space_basis=space_basis, time_modes=time_modes, space_power=space_power, time_power=time_power)


noise_level = 1.0


def reference(readings, space_basis, time_modes, space_power, time_power):
    coefficients = jnp.dot(readings, time_modes, preferred_element_type=jnp.float32).astype(jnp.bfloat16)
    spectral = lax.dot_general(space_basis, coefficients, (((0,), (0,)), ((), ())), preferred_element_type=jnp.float32)
    product = space_power[:, None] * time_power[None, :]
    scaled = (spectral * (product / (product + noise_level))).astype(jnp.bfloat16)
    synthesis = jnp.dot(space_basis, scaled, preferred_element_type=jnp.float32).astype(jnp.bfloat16)
    posterior = lax.dot_general(synthesis, time_modes, (((1,), (1,)), ((), ())), preferred_element_type=jnp.float32)
    return posterior.astype(jnp.bfloat16)
```

```python
import functools

import jax
import jax.numpy as jnp
from jax import lax
from jax.experimental import pallas as pl
from jax.experimental.pallas import tpu as pltpu
from jax.sharding import PartitionSpec as P

MESH = pl.DeviceIdType.MESH
F32, BF16 = jnp.float32, jnp.bfloat16
noise_level = 1.0

CHUNKS = 4
SPACING = 1
X, Y, HOURS = 4, 4, 4

COPIES = dict(hour_sum=3, hour_gather=3, x_gather=3, core_gather=4, y_sum=3, z_sum=1, y_gather=3, core_sum=4, x_sum=3, last_sum=3, last_gather=3)
FIRST = {}
for _name, _count in COPIES.items():
    FIRST[_name] = sum(COPIES[n] for n in FIRST)
TOTAL_COPIES = sum(COPIES.values())


def kernel(
    r_ref, t_ref, b_hbm, space_ref, time_ref, out_ref,
    b, part, part_out, part_in, coef, y_own, y_out, y_in, z_out, z_in, scaled,
    core_out, core_in, own, x_out, x_in, h_own, h_out, h_in, syn,
    send_sem, recv_sem, b_sem,
):
    srow, scol, hour = lax.axis_index("srow"), lax.axis_index("scol"), lax.axis_index("hour")
    low, y = srow // Y, srow % Y
    x, core = scol // 2, scol % 2
    modes = part.shape[2]
    width = b.shape[2]
    sites = r_ref.shape[0]

    def hour_peer(o):
        return (srow, scol, (hour + o) % HOURS)

    def x_peer(o):
        return (srow, ((x + o) % X) * 2 + core, hour)

    def y_peer(o):
        return (low * Y + (y + o) % Y, scol, hour)

    core_peer = (srow, x * 2 + (1 - core), hour)
    low_peer = ((1 - low) * Y + y, scol, hour)

    started = {}

    def send(name, i, q, src, dst, peer):
        at = FIRST[name] + i
        copy = pltpu.make_async_remote_copy(
            src_ref=src, dst_ref=dst, send_sem=send_sem.at[q, at], recv_sem=recv_sem.at[q, at],
            device_id=peer, device_id_type=MESH,
        )
        copy.start()
        started[name, i, q] = copy

    def arrived(name, i, q):
        started[name, i, q].wait_recv()

    def group(c):
        return pl.ds(pl.multiple_of(c * sites, sites), sites)

    barrier = pltpu.get_barrier_semaphore()
    peers = [f(o) for f in (hour_peer, x_peer, y_peer) for o in (1, 2, 3)] + [core_peer, low_peer]
    for peer in peers:
        pl.semaphore_signal(barrier, inc=1, device_id=peer, device_id_type=MESH)
    for j in range(b.shape[0]):
        pltpu.make_async_copy(b_hbm.at[:, pl.ds(j * width, width)], b.at[j], b_sem.at[j]).start()

    def project(q):
        value = lax.dot_general(
            t_ref[:, q * modes : (q + 1) * modes], r_ref[...], (((0,), (1,)), ((), ())), preferred_element_type=F32
        )
        for i in range(HOURS):
            block = value[:, i * modes_sites : (i + 1) * modes_sites]
            part[q, i] = block
            part_out[q, i] = block.astype(BF16)
        if q == 0:
            pl.semaphore_wait(barrier, len(peers))
        for o in (2, 1, 3):
            send("hour_sum", o - 1, q, part_out.at[q, (hour + o) % HOURS], part_in.at[q, o - 1], hour_peer(o))

    modes_sites = part.shape[3]

    def sum_hours(q):
        total = part[q, hour]
        for o in (1, 3, 2):
            arrived("hour_sum", o - 1, q)
            total += part_in[q, o - 1].astype(F32)
        mine = scol * HOURS + hour
        coef[q, mine] = total.astype(BF16)
        for o in (2, 1, 3):
            send("hour_gather", o - 1, q, coef.at[q, mine], coef.at[q, mine], hour_peer(o))

    def gather_x(q):
        for o in (1, 3, 2):
            arrived("hour_gather", o - 1, q)
        mine = coef.at[q, pl.ds(scol * HOURS, HOURS)]
        for o in (2, 1, 3):
            send("x_gather", o - 1, q, mine, mine, x_peer(o))
        send("core_gather", 0, q, mine, mine, core_peer)

    def half(q, j, of_core):
        total = None
        for i in range(X):
            c = i * 2 + of_core
            left = jnp.concatenate([coef[q, c * HOURS + n] for n in range(HOURS)], axis=1)
            term = jnp.dot(left, b[j, group(c), :], preferred_element_type=F32)
            total = term if total is None else total + term
        return total

    def analyse(q):
        for o in (1, 3, 2):
            arrived("x_gather", o - 1, q)
            c = ((x + X - o) % X) * 2 + core
            other = coef.at[q, pl.ds(c * HOURS, HOURS)]
            send("core_gather", o, q, other, other, core_peer)
        if q == 0:
            for j in range(b.shape[0]):
                pltpu.make_async_copy(b_hbm.at[:, pl.ds(j * width, width)], b.at[j], b_sem.at[j]).wait()

        def first(j, carry):
            y_own[q, j] = half(q, j, core)
            return carry

        lax.fori_loop(0, Y, first, 0)
        for i in range(4):
            arrived("core_gather", i, q)

        def second(j, carry):
            total = y_own[q, j] + half(q, j, 1 - core)
            y_own[q, j] = total
            y_out[q, j] = total.astype(BF16)
            return carry

        lax.fori_loop(0, Y, second, 0)
        for o in (2, 1, 3):
            send("y_sum", o - 1, q, y_out.at[q, (y + o) % Y], y_in.at[q, o - 1], y_peer(o))

    def sum_y(q):
        total = y_own[q, y]
        for o in (1, 3, 2):
            arrived("y_sum", o - 1, q)
            total += y_in[q, o - 1].astype(F32)
        y_own[q, y] = total
        z_out[q] = total.astype(BF16)
        send("z_sum", 0, q, z_out.at[q], z_in.at[q], low_peer)

    def scale(q):
        arrived("z_sum", 0, q)
        total = y_own[q, y] + z_in[q].astype(F32)
        product = time_ref[q * modes : (q + 1) * modes, :] * space_ref[y]
        scaled[q, y] = (total * (product / (product + noise_level))).astype(BF16)
        for o in (2, 1, 3):
            send("y_gather", o - 1, q, scaled.at[q, y], scaled.at[q, y], y_peer(o))

    def synthesise(q):
        for o in (1, 3, 2):
            arrived("y_gather", o - 1, q)

        def term(c):
            total = None
            for j in range(Y):
                one = lax.dot_general(
                    scaled[q, j], b[j, group(c), :], (((1,), (1,)), ((), ())), preferred_element_type=F32
                )
                total = one if total is None else total + one
            return total

        for o in (2, 1, 3, 0):
            to = (x + o) % X
            core_out[q, to] = term(to * 2 + (1 - core))
            send("core_sum", o, q, core_out.at[q, to], core_in.at[q, to], core_peer)
        for o in (2, 1, 3, 0):
            to = (x + o) % X
            value = term(to * 2 + core)
            arrived("core_sum", o, q)
            value += core_in[q, to]
            if o:
                x_out[q, to] = value.astype(BF16)
                send("x_sum", o - 1, q, x_out.at[q, to], x_in.at[q, o - 1], x_peer(o))
            else:
                own[q] = value

    def sum_x(q):
        total = own[q]
        for o in (1, 3, 2):
            arrived("x_sum", o - 1, q)
            total += x_in[q, o - 1].astype(F32)
        for i in range(HOURS):
            block = total[:, i * modes_sites : (i + 1) * modes_sites]
            h_own[q, i] = block
            h_out[q, i] = block.astype(BF16)
        for o in (2, 1, 3):
            send("last_sum", o - 1, q, h_out.at[q, (hour + o) % HOURS], h_in.at[q, o - 1], hour_peer(o))

    def sum_last(q):
        total = h_own[q, hour]
        for o in (1, 3, 2):
            arrived("last_sum", o - 1, q)
            total += h_in[q, o - 1].astype(F32)
        mine = syn.at[hour, pl.ds(q * modes, modes)]
        mine[...] = total.astype(BF16)
        for o in (2, 1, 3):
            send("last_gather", o - 1, q, mine, mine, hour_peer(o))

    def finish(q):
        for o in (1, 3, 2):
            arrived("last_gather", o - 1, q)

    stages = [project, sum_hours, gather_x, analyse, sum_y, scale, synthesise, sum_x, sum_last, finish]
    for step in range(len(stages) + SPACING * (CHUNKS - 1)):
        for q in range(CHUNKS):
            at = step - SPACING * q
            if 0 <= at < len(stages):
                stages[at](q)

    def posterior(i, carry):
        value = lax.dot_general(syn[i], t_ref[...], (((0,), (1,)), ((), ())), preferred_element_type=F32)
        out_ref[pl.ds(pl.multiple_of(i * modes_sites, modes_sites), modes_sites), :] = value.astype(out_ref.dtype)
        return carry

    lax.fori_loop(0, HOURS, posterior, 0)
    for copy in started.values():
        copy.wait_send()


def on_device(readings, space_basis, time_modes, space_power, time_power):
    sites, hours = readings.shape
    rows, columns = space_basis.shape
    every_mode = time_modes.shape[1]
    modes, piece, width = every_mode // CHUNKS, sites // HOURS, columns // Y
    groups = rows // sites

    def chunked(dtype, *shape):
        return pltpu.VMEM((CHUNKS, *shape), dtype)

    in_vmem = pl.BlockSpec(memory_space=pltpu.VMEM)
    return pl.pallas_call(
        kernel,
        out_shape=jax.ShapeDtypeStruct((sites, hours), BF16),
        in_specs=[in_vmem, in_vmem, pl.BlockSpec(memory_space=pl.ANY), in_vmem, in_vmem],
        out_specs=in_vmem,
        scratch_shapes=[
            pltpu.VMEM((Y, rows, width), BF16),
            chunked(F32, HOURS, modes, piece),
            chunked(BF16, HOURS, modes, piece),
            chunked(BF16, 3, modes, piece),
            chunked(BF16, groups * HOURS, modes, piece),
            chunked(F32, Y, modes, width),
            chunked(BF16, Y, modes, width),
            chunked(BF16, 3, modes, width),
            chunked(BF16, modes, width),
            chunked(BF16, modes, width),
            chunked(BF16, Y, modes, width),
            chunked(F32, X, modes, sites),
            chunked(F32, X, modes, sites),
            chunked(F32, modes, sites),
            chunked(BF16, X, modes, sites),
            chunked(BF16, 3, modes, sites),
            chunked(F32, HOURS, modes, piece),
            chunked(BF16, HOURS, modes, piece),
            chunked(BF16, 3, modes, piece),
            pltpu.VMEM((HOURS, every_mode, piece), BF16),
            pltpu.SemaphoreType.DMA((CHUNKS, TOTAL_COPIES)),
            pltpu.SemaphoreType.DMA((CHUNKS, TOTAL_COPIES)),
            pltpu.SemaphoreType.DMA((Y,)),
        ],
        compiler_params=pltpu.CompilerParams(
            collective_id=0, has_side_effects=True, vmem_limit_bytes=58 * 2**20
        ),
        name="transform",
    )(readings, time_modes, space_basis, space_power.reshape(Y, 1, width), time_power.reshape(every_mode, 1))


def solution(mesh):
    return jax.shard_map(
        on_device,
        mesh=mesh,
        in_specs=(
            P(("srow", "scol"), "hour"),
            P("srow", ("scol", "hour")),
            P("hour", None),
            P(("scol", "hour")),
            P(),
        ),
        out_specs=P(("srow", "scol"), "hour"),
        check_vma=False,
    )
```

```python
import functools

import jax
import jax.numpy as jnp
from jax import lax
from jax.experimental import pallas as pl
from jax.experimental.pallas import tpu as pltpu
from jax.sharding import PartitionSpec as P

MESH = pl.DeviceIdType.MESH
F32, BF16 = jnp.float32, jnp.bfloat16
noise_level = 1.0

SLICES = ((0, 128), (128, 128), (256, 128), (384, 128))
CHUNKS = len(SLICES)
LANES = 128
X, Y, HOURS = 4, 4, 4

ORDER = (
    (0, 3), (0, 0), (0, 1), (1, 3), (1, 1), (0, 2), (2, 3), (1, 2), (2, 1), (3, 3), (2, 2), (1, 0), (3, 1), (4, 3),
    (2, 0), (5, 3), (4, 1), (3, 2), (5, 1), (6, 3), (3, 0), (4, 2), (6, 1), (5, 2), (4, 0), (7, 3), (5, 0), (6, 2),
    (7, 1), (6, 0), (8, 3), (8, 1), (7, 2), (7, 0), (8, 2), (8, 0), (9, 3), (9, 1), (9, 0), (9, 2),
)

COPIES = dict(hour_sum=3, hour_gather=3, x_gather=3, core_gather=4, y_sum=3, z_sum=1, y_gather=3, core_sum=4, x_sum=3, last_sum=3, last_gather=3)
FIRST = {}
for _name, _count in COPIES.items():
    FIRST[_name] = sum(COPIES[n] for n in FIRST)
TOTAL_COPIES = sum(COPIES.values())


def kernel(
    r_ref, t_ref, b_hbm, space_ref, time_ref, out_ref,
    b, part, part_out, part_in, coef, y_own, y_out, y_in, z_out, z_in, scaled,
    core_out, core_in, own, x_out, x_in, h_own, h_out, h_in, syn, time_columns,
    send_sem, recv_sem, b_sem,
):
    srow, scol, hour = lax.axis_index("srow"), lax.axis_index("scol"), lax.axis_index("hour")
    low, y = srow // Y, srow % Y
    x, core = scol // 2, scol % 2
    width = b.shape[2]
    sites = r_ref.shape[0]
    piece = sites // HOURS

    def hour_peer(o):
        return (srow, scol, (hour + o) % HOURS)

    def x_peer(o):
        return (srow, ((x + o) % X) * 2 + core, hour)

    def y_peer(o):
        return (low * Y + (y + o) % Y, scol, hour)

    core_peer = (srow, x * 2 + (1 - core), hour)
    low_peer = ((1 - low) * Y + y, scol, hour)

    started = {}

    def send(name, i, q, src, dst, peer):
        at = FIRST[name] + i
        copy = pltpu.make_async_remote_copy(
            src_ref=src, dst_ref=dst, send_sem=send_sem.at[q, at], recv_sem=recv_sem.at[q, at],
            device_id=peer, device_id_type=MESH,
        )
        copy.start()
        started[name, i, q] = copy

    def arrived(name, i, q):
        started[name, i, q].wait_recv()

    def group(c):
        return pl.ds(pl.multiple_of(c * sites, sites), sites)

    barrier = pltpu.get_barrier_semaphore()
    peers = [f(o) for f in (hour_peer, x_peer, y_peer) for o in (1, 2, 3)] + [core_peer, low_peer]
    for peer in peers:
        pl.semaphore_signal(barrier, inc=1, device_id=peer, device_id_type=MESH)
    for j in range(b.shape[0]):
        pltpu.make_async_copy(b_hbm.at[:, pl.ds(j * width, width)], b.at[j], b_sem.at[j]).start()

    for i in range(0, time_columns.shape[0], LANES):
        time_columns[i : i + LANES, :] = jnp.broadcast_to(time_ref[:, i : i + LANES], (LANES, LANES)).T

    def project(q):
        value = lax.dot_general(
            t_ref[:, SLICES[q][0] : sum(SLICES[q])], r_ref[...], (((0,), (1,)), ((), ())), preferred_element_type=F32
        )
        for i in range(HOURS):
            block = value[:, i * piece : (i + 1) * piece]
            part[q][i] = block
            part_out[q][i] = block.astype(BF16)
        if q == ORDER[0][1]:
            pl.semaphore_wait(barrier, len(peers))
        for o in (2, 1, 3):
            send("hour_sum", o - 1, q, part_out[q].at[(hour + o) % HOURS], part_in[q].at[o - 1], hour_peer(o))

    def sum_hours(q):
        total = part[q][hour]
        for o in (1, 3, 2):
            arrived("hour_sum", o - 1, q)
            total += part_in[q][o - 1].astype(F32)
        mine = scol * HOURS + hour
        coef[q][mine] = total.astype(BF16)
        for o in (2, 1, 3):
            send("hour_gather", o - 1, q, coef[q].at[mine], coef[q].at[mine], hour_peer(o))

    def gather_x(q):
        for o in (1, 3, 2):
            arrived("hour_gather", o - 1, q)
        mine = coef[q].at[pl.ds(scol * HOURS, HOURS)]
        for o in (2, 1, 3):
            send("x_gather", o - 1, q, mine, mine, x_peer(o))
        send("core_gather", 0, q, mine, mine, core_peer)

    def half(q, j, of_core):
        total = None
        for i in range(X):
            c = i * 2 + of_core
            left = jnp.concatenate([coef[q][c * HOURS + n] for n in range(HOURS)], axis=1)
            term = jnp.dot(left, b[j, group(c), :], preferred_element_type=F32)
            total = term if total is None else total + term
        return total

    def analyse(q):
        for o in (1, 3, 2):
            arrived("x_gather", o - 1, q)
            c = ((x + X - o) % X) * 2 + core
            other = coef[q].at[pl.ds(c * HOURS, HOURS)]
            send("core_gather", o, q, other, other, core_peer)
        if (3, q) == next(o for o in ORDER if o[0] == 3):
            for j in range(b.shape[0]):
                pltpu.make_async_copy(b_hbm.at[:, pl.ds(j * width, width)], b.at[j], b_sem.at[j]).wait()

        def first(j, carry):
            y_own[q][j] = half(q, j, core)
            return carry

        lax.fori_loop(0, Y, first, 0)
        for i in range(4):
            arrived("core_gather", i, q)

        def second(j, carry):
            total = y_own[q][j] + half(q, j, 1 - core)
            y_own[q][j] = total
            y_out[q][j] = total.astype(BF16)
            return carry

        lax.fori_loop(0, Y, second, 0)
        for o in (2, 1, 3):
            send("y_sum", o - 1, q, y_out[q].at[(y + o) % Y], y_in[q].at[o - 1], y_peer(o))

    def sum_y(q):
        total = y_own[q][y]
        for o in (1, 3, 2):
            arrived("y_sum", o - 1, q)
            total += y_in[q][o - 1].astype(F32)
        y_own[q][y] = total
        z_out[q][...] = total.astype(BF16)
        send("z_sum", 0, q, z_out[q], z_in[q], low_peer)

    def scale(q):
        time = time_columns[SLICES[q][0] : sum(SLICES[q]), :]
        product = jnp.concatenate([time] * (width // LANES), axis=1) * space_ref[y]
        ratio = product / (product + noise_level)
        arrived("z_sum", 0, q)
        total = y_own[q][y] + z_in[q][...].astype(F32)
        scaled[q][y] = (total * ratio).astype(BF16)
        for o in (2, 1, 3):
            send("y_gather", o - 1, q, scaled[q].at[y], scaled[q].at[y], y_peer(o))

    def synthesise(q):
        for o in (1, 3, 2):
            arrived("y_gather", o - 1, q)

        def term(c):
            total = None
            for j in range(Y):
                one = lax.dot_general(
                    scaled[q][j], b[j, group(c), :], (((1,), (1,)), ((), ())), preferred_element_type=F32
                )
                total = one if total is None else total + one
            return total

        for o in (2, 1, 3, 0):
            to = (x + o) % X
            core_out[q][to] = term(to * 2 + (1 - core))
            send("core_sum", o, q, core_out[q].at[to], core_in[q].at[to], core_peer)
        for o in (2, 1, 3, 0):
            to = (x + o) % X
            value = term(to * 2 + core)
            arrived("core_sum", o, q)
            value += core_in[q][to]
            if o:
                x_out[q][to] = value.astype(BF16)
                send("x_sum", o - 1, q, x_out[q].at[to], x_in[q].at[o - 1], x_peer(o))
            else:
                own[q][...] = value

    def sum_x(q):
        total = own[q][...]
        for o in (1, 3, 2):
            arrived("x_sum", o - 1, q)
            total += x_in[q][o - 1].astype(F32)
        for i in range(HOURS):
            block = total[:, i * piece : (i + 1) * piece]
            h_own[q][i] = block
            h_out[q][i] = block.astype(BF16)
        for o in (2, 1, 3):
            send("last_sum", o - 1, q, h_out[q].at[(hour + o) % HOURS], h_in[q].at[o - 1], hour_peer(o))

    def sum_last(q):
        total = h_own[q][hour]
        for o in (1, 3, 2):
            arrived("last_sum", o - 1, q)
            total += h_in[q][o - 1].astype(F32)
        mine = syn.at[hour, pl.ds(*SLICES[q])]
        mine[...] = total.astype(BF16)
        for o in (2, 1, 3):
            send("last_gather", o - 1, q, mine, mine, hour_peer(o))

    def finish(q):
        for o in (1, 3, 2):
            arrived("last_gather", o - 1, q)

    stages = [project, sum_hours, gather_x, analyse, sum_y, scale, synthesise, sum_x, sum_last, finish]
    for at, q in ORDER:
        stages[at](q)

    out_ref[...] = syn[...]
    for copy in started.values():
        copy.wait_send()


def on_device(readings, space_basis, time_modes, space_power, time_power):
    sites, hours = readings.shape
    rows, columns = space_basis.shape
    every_mode = time_modes.shape[1]
    piece, width = sites // HOURS, columns // Y
    groups = rows // sites

    def chunked(dtype, *shape):
        return [pltpu.VMEM((*shape[:-1], modes, shape[-1]), dtype) for _, modes in SLICES]

    in_vmem = pl.BlockSpec(memory_space=pltpu.VMEM)
    synthesis = pl.pallas_call(
        kernel,
        out_shape=jax.ShapeDtypeStruct((HOURS, every_mode, piece), BF16),
        in_specs=[in_vmem, in_vmem, pl.BlockSpec(memory_space=pl.ANY), in_vmem, in_vmem],
        out_specs=in_vmem,
        scratch_shapes=[
            pltpu.VMEM((Y, rows, width), BF16),
            chunked(F32, HOURS, piece),
            chunked(BF16, HOURS, piece),
            chunked(BF16, 3, piece),
            chunked(BF16, groups * HOURS, piece),
            chunked(F32, Y, width),
            chunked(BF16, Y, width),
            chunked(BF16, 3, width),
            chunked(BF16, width),
            chunked(BF16, width),
            chunked(BF16, Y, width),
            chunked(F32, X, sites),
            chunked(F32, X, sites),
            chunked(F32, sites),
            chunked(BF16, X, sites),
            chunked(BF16, 3, sites),
            chunked(F32, HOURS, piece),
            chunked(BF16, HOURS, piece),
            chunked(BF16, 3, piece),
            pltpu.VMEM((HOURS, every_mode, piece), BF16),
            pltpu.VMEM((every_mode, LANES), F32),
            pltpu.SemaphoreType.DMA((CHUNKS, TOTAL_COPIES)),
            pltpu.SemaphoreType.DMA((CHUNKS, TOTAL_COPIES)),
            pltpu.SemaphoreType.DMA((Y,)),
        ],
        compiler_params=pltpu.CompilerParams(
            collective_id=0, has_side_effects=True, vmem_limit_bytes=58 * 2**20
        ),
        name="transform",
    )(readings, time_modes, space_basis, space_power.reshape(Y, 1, width), time_power.reshape(1, every_mode))
    posterior = jnp.einsum('hms,tm->hst', synthesis, time_modes, preferred_element_type=F32)
    return posterior.reshape(sites, hours).astype(BF16)


def solution(mesh):
    return jax.shard_map(
        on_device,
        mesh=mesh,
        in_specs=(
            P(("srow", "scol"), "hour"),
            P("srow", ("scol", "hour")),
            P("hour", None),
            P(("scol", "hour")),
            P(),
        ),
        out_specs=P(("srow", "scol"), "hour"),
        check_vma=False,
    )
```

```python
import functools

import jax
import jax.numpy as jnp
from jax import lax
from jax.experimental import pallas as pl
from jax.experimental.pallas import tpu as pltpu
from jax.sharding import PartitionSpec as P

MESH = pl.DeviceIdType.MESH
F32, BF16 = jnp.float32, jnp.bfloat16
noise_level = 1.0

SLICES = ((0, 128), (128, 128), (256, 128), (384, 128))
CHUNKS = len(SLICES)
LANES = 128
X, Y, HOURS = 4, 4, 4

ORDER = (
    (0, 1), (0, 3), (0, 0), (1, 1), (1, 0), (0, 2), (2, 1), (1, 3), (2, 0), (1, 2), (3, 1), (2, 2), (3, 0), (4, 1),
    (2, 3), (5, 1), (4, 0), (3, 2), (5, 0), (6, 1), (3, 3), (4, 2), (6, 0), (5, 2), (4, 3), (7, 1), (5, 3), (6, 2),
    (7, 0), (6, 3), (8, 1), (8, 0), (7, 2), (9, 1), (7, 3), (8, 2), (9, 0), (8, 3), (9, 3), (9, 2),
)

COPIES = dict(hour_sum=3, hour_gather=3, x_gather=3, core_gather=4, y_sum=3, z_sum=1, y_gather=3, core_sum=4, x_sum=3, last_sum=3, last_gather=3)
FIRST = {}
for _name, _count in COPIES.items():
    FIRST[_name] = sum(COPIES[n] for n in FIRST)
TOTAL_COPIES = sum(COPIES.values())


def kernel(
    r_ref, t_ref, b_hbm, space_ref, time_ref, out_hbm,
    b, part, part_out, part_in, coef, y_own, y_out, y_in, z_out, z_in, scaled,
    core_out, core_in, own, x_out, x_in, h_own, h_out, h_in, syn, time_columns,
    send_sem, recv_sem, b_sem, out_sem,
):
    srow, scol, hour = lax.axis_index("srow"), lax.axis_index("scol"), lax.axis_index("hour")
    low, y = srow // Y, srow % Y
    x, core = scol // 2, scol % 2
    width = b.shape[2]
    sites = r_ref.shape[0]
    piece = sites // HOURS

    def hour_peer(o):
        return (srow, scol, (hour + o) % HOURS)

    def x_peer(o):
        return (srow, ((x + o) % X) * 2 + core, hour)

    def y_peer(o):
        return (low * Y + (y + o) % Y, scol, hour)

    core_peer = (srow, x * 2 + (1 - core), hour)
    low_peer = ((1 - low) * Y + y, scol, hour)

    started = {}

    def send(name, i, q, src, dst, peer):
        at = FIRST[name] + i
        copy = pltpu.make_async_remote_copy(
            src_ref=src, dst_ref=dst, send_sem=send_sem.at[q, at], recv_sem=recv_sem.at[q, at],
            device_id=peer, device_id_type=MESH,
        )
        copy.start()
        started[name, i, q] = copy

    def arrived(name, i, q):
        started[name, i, q].wait_recv()

    def group(c):
        return pl.ds(pl.multiple_of(c * sites, sites), sites)

    barrier = pltpu.get_barrier_semaphore()
    peers = [f(o) for f in (hour_peer, x_peer, y_peer) for o in (1, 2, 3)] + [core_peer, low_peer]
    for peer in peers:
        pl.semaphore_signal(barrier, inc=1, device_id=peer, device_id_type=MESH)
    for j in range(b.shape[0]):
        pltpu.make_async_copy(b_hbm.at[:, pl.ds(j * width, width)], b.at[j], b_sem.at[j]).start()

    for i in range(0, time_columns.shape[0], LANES):
        time_columns[i : i + LANES, :] = jnp.broadcast_to(time_ref[:, i : i + LANES], (LANES, LANES)).T

    def project(q):
        value = lax.dot_general(
            t_ref[:, SLICES[q][0] : sum(SLICES[q])], r_ref[...], (((0,), (1,)), ((), ())), preferred_element_type=F32
        )
        for i in range(HOURS):
            block = value[:, i * piece : (i + 1) * piece]
            part[q][i] = block
            part_out[q][i] = block.astype(BF16)
        if q == ORDER[0][1]:
            pl.semaphore_wait(barrier, len(peers))
        for o in (2, 1, 3):
            send("hour_sum", o - 1, q, part_out[q].at[(hour + o) % HOURS], part_in[q].at[o - 1], hour_peer(o))

    def sum_hours(q):
        total = part[q][hour]
        for o in (1, 3, 2):
            arrived("hour_sum", o - 1, q)
            total += part_in[q][o - 1].astype(F32)
        mine = scol * HOURS + hour
        coef[q][mine] = total.astype(BF16)
        for o in (2, 1, 3):
            send("hour_gather", o - 1, q, coef[q].at[mine], coef[q].at[mine], hour_peer(o))

    def gather_x(q):
        for o in (1, 3, 2):
            arrived("hour_gather", o - 1, q)
        mine = coef[q].at[pl.ds(scol * HOURS, HOURS)]
        for o in (2, 1, 3):
            send("x_gather", o - 1, q, mine, mine, x_peer(o))
        send("core_gather", 0, q, mine, mine, core_peer)

    def half(q, j, of_core):
        total = None
        for i in range(X):
            c = i * 2 + of_core
            left = jnp.concatenate([coef[q][c * HOURS + n] for n in range(HOURS)], axis=1)
            term = jnp.dot(left, b[j, group(c), :], preferred_element_type=F32)
            total = term if total is None else total + term
        return total

    def analyse(q):
        for o in (1, 3, 2):
            arrived("x_gather", o - 1, q)
            c = ((x + X - o) % X) * 2 + core
            other = coef[q].at[pl.ds(c * HOURS, HOURS)]
            send("core_gather", o, q, other, other, core_peer)
        if (3, q) == next(o for o in ORDER if o[0] == 3):
            for j in range(b.shape[0]):
                pltpu.make_async_copy(b_hbm.at[:, pl.ds(j * width, width)], b.at[j], b_sem.at[j]).wait()

        def first(j, carry):
            y_own[q][j] = half(q, j, core)
            return carry

        lax.fori_loop(0, Y, first, 0)
        for i in range(4):
            arrived("core_gather", i, q)

        def second(j, carry):
            total = y_own[q][j] + half(q, j, 1 - core)
            y_own[q][j] = total
            y_out[q][j] = total.astype(BF16)
            return carry

        lax.fori_loop(0, Y, second, 0)
        for o in (2, 1, 3):
            send("y_sum", o - 1, q, y_out[q].at[(y + o) % Y], y_in[q].at[o - 1], y_peer(o))

    def sum_y(q):
        total = y_own[q][y]
        for o in (1, 3, 2):
            arrived("y_sum", o - 1, q)
            total += y_in[q][o - 1].astype(F32)
        y_own[q][y] = total
        z_out[q][...] = total.astype(BF16)
        send("z_sum", 0, q, z_out[q], z_in[q], low_peer)

    def scale(q):
        time = time_columns[SLICES[q][0] : sum(SLICES[q]), :]
        product = jnp.concatenate([time] * (width // LANES), axis=1) * space_ref[y]
        ratio = product / (product + noise_level)
        arrived("z_sum", 0, q)
        total = y_own[q][y] + z_in[q][...].astype(F32)
        scaled[q][y] = (total * ratio).astype(BF16)
        for o in (2, 1, 3):
            send("y_gather", o - 1, q, scaled[q].at[y], scaled[q].at[y], y_peer(o))

    def synthesise(q):
        for o in (1, 3, 2):
            arrived("y_gather", o - 1, q)

        def term(c):
            total = None
            for j in range(Y):
                one = lax.dot_general(
                    scaled[q][j], b[j, group(c), :], (((1,), (1,)), ((), ())), preferred_element_type=F32
                )
                total = one if total is None else total + one
            return total

        for o in (2, 1, 3, 0):
            to = (x + o) % X
            core_out[q][to] = term(to * 2 + (1 - core)).astype(BF16)
            send("core_sum", o, q, core_out[q].at[to], core_in[q].at[to], core_peer)
        for o in (2, 1, 3, 0):
            to = (x + o) % X
            value = term(to * 2 + core)
            arrived("core_sum", o, q)
            value += core_in[q][to].astype(F32)
            if o:
                x_out[q][to] = value.astype(BF16)
                send("x_sum", o - 1, q, x_out[q].at[to], x_in[q].at[o - 1], x_peer(o))
            else:
                own[q][...] = value

    def sum_x(q):
        total = own[q][...]
        for o in (1, 3, 2):
            arrived("x_sum", o - 1, q)
            total += x_in[q][o - 1].astype(F32)
        for i in range(HOURS):
            block = total[:, i * piece : (i + 1) * piece]
            h_own[q][i] = block
            h_out[q][i] = block.astype(BF16)
        for o in (2, 1, 3):
            send("last_sum", o - 1, q, h_out[q].at[(hour + o) % HOURS], h_in[q].at[o - 1], hour_peer(o))

    def sum_last(q):
        total = h_own[q][hour]
        for o in (1, 3, 2):
            arrived("last_sum", o - 1, q)
            total += h_in[q][o - 1].astype(F32)
        mine = syn.at[hour, pl.ds(*SLICES[q])]
        mine[...] = total.astype(BF16)
        for o in (2, 1, 3):
            send("last_gather", o - 1, q, mine, mine, hour_peer(o))

    def finish(q):
        for o in (1, 3, 2):
            arrived("last_gather", o - 1, q)
        done = syn.at[:, pl.ds(*SLICES[q])]
        stored.append(pltpu.make_async_copy(done, out_hbm.at[:, pl.ds(*SLICES[q])], out_sem.at[q]))
        stored[-1].start()

    stored = []

    stages = [project, sum_hours, gather_x, analyse, sum_y, scale, synthesise, sum_x, sum_last, finish]
    for at, q in ORDER:
        stages[at](q)

    for copy in started.values():
        copy.wait_send()
    for copy in stored:
        copy.wait()


def on_device(readings, space_basis, time_modes, space_power, time_power):
    sites, hours = readings.shape
    rows, columns = space_basis.shape
    every_mode = time_modes.shape[1]
    piece, width = sites // HOURS, columns // Y
    groups = rows // sites

    def chunked(dtype, *shape):
        return [pltpu.VMEM((*shape[:-1], modes, shape[-1]), dtype) for _, modes in SLICES]

    in_vmem = pl.BlockSpec(memory_space=pltpu.VMEM)
    synthesis = pl.pallas_call(
        kernel,
        out_shape=jax.ShapeDtypeStruct((HOURS, every_mode, piece), BF16),
        in_specs=[in_vmem, in_vmem, pl.BlockSpec(memory_space=pl.ANY), in_vmem, in_vmem],
        out_specs=pl.BlockSpec(memory_space=pl.ANY),
        scratch_shapes=[
            pltpu.VMEM((Y, rows, width), BF16),
            chunked(F32, HOURS, piece),
            chunked(BF16, HOURS, piece),
            chunked(BF16, 3, piece),
            chunked(BF16, groups * HOURS, piece),
            chunked(F32, Y, width),
            chunked(BF16, Y, width),
            chunked(BF16, 3, width),
            chunked(BF16, width),
            chunked(BF16, width),
            chunked(BF16, Y, width),
            chunked(BF16, X, sites),
            chunked(BF16, X, sites),
            chunked(F32, sites),
            chunked(BF16, X, sites),
            chunked(BF16, 3, sites),
            chunked(F32, HOURS, piece),
            chunked(BF16, HOURS, piece),
            chunked(BF16, 3, piece),
            pltpu.VMEM((HOURS, every_mode, piece), BF16),
            pltpu.VMEM((every_mode, LANES), F32),
            pltpu.SemaphoreType.DMA((CHUNKS, TOTAL_COPIES)),
            pltpu.SemaphoreType.DMA((CHUNKS, TOTAL_COPIES)),
            pltpu.SemaphoreType.DMA((Y,)),
            pltpu.SemaphoreType.DMA((CHUNKS,)),
        ],
        compiler_params=pltpu.CompilerParams(
            collective_id=0, has_side_effects=True, vmem_limit_bytes=58 * 2**20
        ),
        name="transform",
    )(readings, time_modes, space_basis, space_power.reshape(Y, 1, width), time_power.reshape(1, every_mode))
    posterior = jnp.einsum('hms,tm->hst', synthesis, time_modes, preferred_element_type=F32)
    return posterior.reshape(sites, hours).astype(BF16)


def solution(mesh):
    return jax.shard_map(
        on_device,
        mesh=mesh,
        in_specs=(
            P(("srow", "scol"), "hour"),
            P("srow", ("scol", "hour")),
            P("hour", None),
            P(("scol", "hour")),
            P(),
        ),
        out_specs=P(("srow", "scol"), "hour"),
        check_vma=False,
    )
```
